32 devices in a mesh: pair: 4 (over y, x), virt: 8 (over z, core).
Axes of the slice: x: 2, y: 2, z: 4, core: 2. Of those that a mesh axis runs over, the one named last changes fastest.
Arguments:
- amplitudes: float32 [2048, 16384], P('pair', 'virt'), may hold values from -6 to 6
- integrals: bfloat16 [16384, 16384], P('pair', 'virt'), may hold values from -0.046875 to 0.046875
- occ_energy: float32 [2048], P('pair'), may hold values from 0.5 to 4
- vir_energy: float32 [16384], P('virt'), may hold values from 0.5 to 4
- tile_mask: int32 [256, 128], P('pair', 'virt'), may hold values 0 or 1
- partner_slot: int32 [256, 128], P('pair', 'virt'), may hold values from 0 to 31, as said below
Outputs:
- new_amplitudes: float32 [2048, 16384], P('pair', 'virt')
The draws below stay inside these ranges and needn't reach their ends.
Inputs may be any that keep to these rules, and one draw needn't show every extreme that they name: `partner_slot`: within the block of tiles of each device (tile rows of one pair index by tile columns of one virt index), every device number 0 to 31 stands exactly 32 times, in an order drawn from the seed.
All inputs are finite; a program needn't handle non-finite values. No bound on the sum of `tile_mask` on one device may be relied on, other than what follows from the above.
Results may differ from the reference program's by a relative error of at most 0.0012.
Values may be sent and summed in bfloat16 or wider, within the bound.
A program may use at most 128 MiB of HBM per device.

```python
import math
import jax
import jax.numpy as jnp
from jax import lax

VIR = 16384
TR = 8
TC = 128
OCC = 2048
COLS = 2048
NRT = 256
NCT = 128
RT_DEV = 64
CT_DEV = 16
TILES_DEV = 1024
PER_PEER = 32
N_PAIR = 4
N_VIRT = 8
DEVICES = 32


def draw_partner_slot(key, part):
    base_slots = jnp.tile(jnp.arange(DEVICES, dtype=jnp.int32), PER_PEER)
    sub_keys = jax.random.split(key, DEVICES)

    def shuffled(sub_key):
        return base_slots[jax.random.permutation(sub_key, TILES_DEV)]
    device_slots = jax.vmap(shuffled)(sub_keys)
    arranged = device_slots.reshape(N_PAIR, N_VIRT, RT_DEV, CT_DEV).transpose(0, 2, 1, 3)
    return arranged.reshape(NRT, NCT).astype(jnp.int32)


def place_ends(drawn, stream_key, low, largest):
    dims = drawn.shape
    spot = [jax.random.randint(jax.random.fold_in(stream_key, axis), (), 0, dims[axis]) for axis in range(len(dims))]
    drawn = drawn.at[tuple(spot)].set(low)
    longest = dims.index(max(dims))
    spot[longest] = (spot[longest] + 1) % dims[longest]
    return drawn.at[tuple(spot)].set(largest)


def block_scale(own_key, shape, cuts, smallest, high):
    loudness = 1.0
    for dim, shards_of in cuts:
        heights = jax.random.uniform(jax.random.fold_in(jax.random.fold_in(own_key, 6), dim), (shards_of,), jnp.float32, smallest / len(cuts), high / len(cuts))
        loudness = loudness * jnp.repeat(jnp.exp(heights), shape[dim] // shards_of).reshape((-1,) + (1,) * (len(shape) - 1 - dim))
    return loudness


def gaussian(stream_key, shape, spread, reach, cuts=(), held_as=jnp.bfloat16):
    result = jax.random.normal(stream_key, shape, jnp.float32) * spread
    if len(cuts) > 0:
        result = block_scale(stream_key, shape, cuts, -0.22, 0.18) * result
    return jnp.clip(result, min=-reach, max=reach).astype(held_as)


def setup_inputs(seed: int = 0) -> dict:
    keys = jax.random.split(jax.random.key(seed), 7)
    return {
        "amplitudes": gaussian(keys[0], (OCC, VIR), 1.0, 6.0, ((0, 4), (1, 8)), jnp.float32),
        "integrals": gaussian(keys[1], (VIR, VIR), VIR ** -0.5, 0.046875, ((0, 4), (1, 8))),
        "occ_energy": jnp.clip(jnp.exp(math.log(4.0) - 2.0794415 * jax.random.uniform(keys[2], (OCC,), jnp.float32) ** block_scale(keys[2], (OCC,), ((0, 4),), -0.2, 0.2)), 0.5, 4.0),
        "vir_energy": jnp.clip(jnp.exp(math.log(4.0) - 2.0794415 * jax.random.uniform(keys[3], (VIR,), jnp.float32) ** block_scale(keys[3], (VIR,), ((0, 8),), -0.2, 0.2)), 0.5, 4.0),
        "tile_mask": place_ends((jax.random.randint(keys[4], (NRT, NCT), 0, 4) < 3).astype(jnp.int32), jax.random.fold_in(keys[4], 1), 0, 1),
        "partner_slot": draw_partner_slot(jax.random.fold_in(keys[6], 71), 0),
    }


def reference(amplitudes, integrals, occ_energy, vir_energy, tile_mask, partner_slot):
    amp_half = amplitudes.astype(jnp.bfloat16)
    blocks = integrals.reshape(VIR, N_VIRT, COLS).transpose(1, 0, 2)

    def column_block(block):
        return jnp.dot(amp_half, block, preferred_element_type=jnp.float32)

    product = lax.map(column_block, blocks)
    ladder = product.transpose(1, 0, 2).reshape(OCC, VIR)
    weights = tile_mask.astype(jnp.float32)
    masked = ladder.reshape(NRT, TR, NCT, TC) * weights[:, None, :, None]
    tiles = masked.reshape(N_PAIR, RT_DEV, TR, N_VIRT, CT_DEV, TC).transpose(0, 3, 1, 4, 2, 5).reshape(DEVICES, TILES_DEV, TR * TC)
    slots = partner_slot.reshape(N_PAIR, RT_DEV, N_VIRT, CT_DEV).transpose(0, 2, 1, 3).reshape(DEVICES, TILES_DEV)
    ordering = jnp.argsort(slots, axis=1, stable=True).astype(jnp.int32)
    inverse = jnp.argsort(ordering, axis=1, stable=True).astype(jnp.int32)
    outgoing = jnp.take_along_axis(tiles, ordering[:, :, None], axis=1).reshape(DEVICES, DEVICES, PER_PEER, TR * TC)
    incoming = outgoing.transpose(1, 0, 2, 3).reshape(DEVICES, TILES_DEV, TR * TC)
    partner = jnp.take_along_axis(incoming, inverse[:, :, None], axis=1)
    symmetric = (tiles + partner).reshape(N_PAIR, N_VIRT, RT_DEV, CT_DEV, TR, TC).transpose(0, 2, 4, 1, 3, 5).reshape(OCC, VIR)
    denominator = occ_energy[:, None] + vir_energy[None, :]
    return amplitudes - symmetric / denominator
```

```python
import functools
import jax
import jax.numpy as jnp
from jax import lax
from jax.experimental import pallas as pl
from jax.experimental.pallas import tpu as pltpu
from jax.sharding import PartitionSpec as P

TR = 8
TC = 128
CHUNK = 64
LAG_CORE = 1
LAG_DOT = 2
LAG_SUM = 4
WIRE = jnp.bfloat16
TILE_WIRE = jnp.float16
MESH = pl.DeviceIdType.MESH


def ladder_kernel(
    pairs, virts, chunks, rows, tile_n,
    amp_ref, int_ref, out_ref, chain_ref,
    weights, gathered, part_out, part_in,
    weight_sem, chain_send, chain_recv, plane_send, plane_recv,
    core_send, core_recv, part_send, part_recv,
):
    share = virts // pairs
    spots = pairs
    p = lax.axis_index("pair")
    v = lax.axis_index("virt")
    u = v // share
    c = v % share
    depth = amp_ref.shape[1]
    width = int_ref.shape[1]

    load = pltpu.make_async_copy(int_ref, weights, weight_sem)
    load.start()

    barrier = pltpu.get_barrier_semaphore()

    def greet(pp, vv):
        pl.semaphore_signal(barrier, inc=1, device_id=(pp, vv), device_id_type=MESH)

    for k in range(1, pairs):
        greet((p + k) % pairs, v)
    for k in range(1, share):
        greet(p, u * share + (c + k) % share)

    for k in range(1, spots):
        greet(p, (u + k) % spots * share + c)

    pl.semaphore_wait(barrier, pairs - 1 + share - 1 + spots - 1)

    def piece(r):
        return pl.ds(pl.multiple_of(r * rows, rows), rows)

    def chain_copy(src, w, r, up):
        return pltpu.make_async_remote_copy(
            src_ref=src,
            dst_ref=chain_ref.at[w, piece(r)],
            send_sem=chain_send.at[up, w, r],
            recv_sem=chain_recv.at[w, r],
            device_id=(p, v + share if up else v - share),
            device_id_type=MESH,
        )

    def plane_copy(src, w, r):
        return pltpu.make_async_remote_copy(
            src_ref=src,
            dst_ref=gathered.at[c, r, p],
            send_sem=plane_send.at[w, r],
            recv_sem=plane_recv.at[p, r],
            device_id=(w, v),
            device_id_type=MESH,
        )

    def keep_copy(src, r):
        return pltpu.make_async_copy(src, gathered.at[c, r, p], plane_recv.at[p, r])

    def pass_on(src, w, r):
        @pl.when(w != p)
        def _():
            plane_copy(src, w, r).start()

        @pl.when(w == p)
        def _():
            keep_copy(src, r).start()

    def core_copy(k, r):
        return pltpu.make_async_remote_copy(
            src_ref=gathered.at[c, r],
            dst_ref=gathered.at[c, r],
            send_sem=core_send.at[k, r],
            recv_sem=core_recv.at[k, r],
            device_id=(p, u * share + (c + k) % share),
            device_id_type=MESH,
        )

    def part_copy(q, r):
        return pltpu.make_async_remote_copy(
            src_ref=part_out.at[r, q],
            dst_ref=part_in.at[r, p],
            send_sem=part_send.at[q, r],
            recv_sem=part_recv.at[p, r],
            device_id=(q, v),
            device_id_type=MESH,
        )

    def spread(r):
        mine = amp_ref.at[piece(r)]

        @pl.when(u > 0)
        def _():
            chain_copy(mine, u, r, 0).start()

        @pl.when(u < spots - 1)
        def _():
            chain_copy(mine, u, r, 1).start()

        pass_on(mine, u, r)
        for d in range(1, spots):
            low = u - d
            high = u + d

            @pl.when(low >= 0)
            def _():
                chain_copy(mine, low, r, 1).wait_recv()
                block = chain_ref.at[low, piece(r)]

                @pl.when(u < spots - 1)
                def _():
                    chain_copy(block, low, r, 1).start()

                pass_on(block, low, r)

            @pl.when(high < spots)
            def _():
                chain_copy(mine, high, r, 0).wait_recv()
                block = chain_ref.at[high, piece(r)]

                @pl.when(u > 0)
                def _():
                    chain_copy(block, high, r, 0).start()

                pass_on(block, high, r)

    def swap(r):
        keep_copy(amp_ref.at[piece(r)], r).wait()
        for k in range(1, pairs):
            q = (p + k) % pairs
            pltpu.make_async_remote_copy(
                src_ref=amp_ref.at[piece(r)],
                dst_ref=gathered.at[c, r, q],
                send_sem=plane_send.at[q, r],
                recv_sem=plane_recv.at[q, r],
                device_id=(q, v),
                device_id_type=MESH,
            ).wait_recv()
        for k in range(1, share):
            core_copy(k, r).start()

    def multiply(r):
        for k in range(1, share):
            pltpu.make_async_remote_copy(
                src_ref=gathered.at[c, r],
                dst_ref=gathered.at[(c + share - k) % share, r],
                send_sem=core_send.at[k, r],
                recv_sem=core_recv.at[k, r],
                device_id=(p, u * share + (c + share - k) % share),
                device_id_type=MESH,
            ).wait_recv()

        @pl.when(r == 0)
        def _():
            load.wait()

        def columns(n, carry):
            cut = pl.ds(pl.multiple_of(n * tile_n, tile_n), tile_n)
            total = jnp.zeros((pairs * rows, tile_n), jnp.float32)
            for s in range(share):
                total = total + jnp.dot(
                    gathered[s, r].reshape(pairs * rows, depth),
                    weights[s * depth : (s + 1) * depth, cut],
                    preferred_element_type=jnp.float32,
                )
            for q in range(pairs):
                part = total[q * rows : (q + 1) * rows]
                part_out[r, q, :, cut] = part.astype(WIRE)

                @pl.when(q == p)
                def _():
                    out_ref[piece(r), cut] = part
            return carry

        lax.fori_loop(0, width // tile_n, columns, 0)
        for k in range(1, pairs):
            part_copy((p + k) % pairs, r).start()

    def collect(r):
        for k in range(1, pairs):
            q = (p + k) % pairs
            pltpu.make_async_remote_copy(
                src_ref=part_out.at[r, q],
                dst_ref=part_in.at[r, q],
                send_sem=part_send.at[q, r],
                recv_sem=part_recv.at[q, r],
                device_id=(q, v),
                device_id_type=MESH,
            ).wait_recv()
        total = out_ref[piece(r), :]
        for k in range(1, pairs):
            total = total + part_in[r, (p + k) % pairs].astype(jnp.float32)
        out_ref[piece(r), :] = total

    def step(s, carry):
        @pl.when(s < chunks)
        def _():
            spread(s)

        @pl.when((s >= LAG_CORE) & (s < chunks + LAG_CORE))
        def _():
            swap(s - LAG_CORE)

        @pl.when((s >= LAG_DOT) & (s < chunks + LAG_DOT))
        def _():
            multiply(s - LAG_DOT)

        @pl.when(s >= LAG_SUM)
        def _():
            collect(s - LAG_SUM)

        return carry

    lax.fori_loop(0, chunks + LAG_SUM, step, 0)

    def drain(r, carry):
        mine = amp_ref.at[piece(r)]
        for w in range(spots):
            @pl.when((u > 0) & (w >= u))
            def _():
                chain_copy(mine, w, r, 0).wait_send()

            @pl.when((u < spots - 1) & (w <= u))
            def _():
                chain_copy(mine, w, r, 1).wait_send()

            @pl.when(w != p)
            def _():
                plane_copy(mine, w, r).wait_send()
                part_copy(w, r).wait_send()
        for k in range(1, share):
            core_copy(k, r).wait_send()
        return carry

    lax.fori_loop(0, chunks, drain, 0)


def ladder_block(amp_half, integrals, pairs, virts):
    row_count, depth = amp_half.shape
    width = integrals.shape[1]
    rows = min(CHUNK, row_count)
    chunks = row_count // rows
    share = virts // pairs
    tile_n = min(256, width)
    dma = pltpu.SemaphoreType.DMA
    ladder, _ = pl.pallas_call(
        functools.partial(ladder_kernel, pairs, virts, chunks, rows, tile_n),
        out_shape=(
            jax.ShapeDtypeStruct((row_count, width), jnp.float32),
            jax.ShapeDtypeStruct((pairs, row_count, depth), jnp.bfloat16),
        ),
        in_specs=[pl.BlockSpec(memory_space=pl.ANY)] * 2,
        out_specs=(
            pl.BlockSpec(memory_space=pltpu.VMEM),
            pl.BlockSpec(memory_space=pl.ANY),
        ),
        scratch_shapes=[
            pltpu.VMEM(integrals.shape, jnp.bfloat16),
            pltpu.VMEM((share, chunks, pairs, rows, depth), jnp.bfloat16),
            pltpu.VMEM((chunks, pairs, rows, width), WIRE),
            pltpu.VMEM((chunks, pairs, rows, width), WIRE),
            dma(()),
            dma((2, pairs, chunks)),
            dma((pairs, chunks)),
            dma((pairs, chunks)),
            dma((pairs, chunks)),
            dma((share, chunks)),
            dma((share, chunks)),
            dma((pairs, chunks)),
            dma((pairs, chunks)),
        ],
        compiler_params=pltpu.CompilerParams(
            collective_id=0, has_side_effects=True, vmem_limit_bytes=60 * 2**20
        ),
        cost_estimate=pl.CostEstimate(
            flops=2 * pairs * row_count * share * depth * width,
            bytes_accessed=2 * integrals.size + 8 * amp_half.size,
            transcendentals=0,
        ),
    )(amp_half, integrals)
    return ladder


def shards(amplitudes, integrals, occ_energy, vir_energy, tile_mask, partner_slot):
    row_count, col_count = amplitudes.shape
    pair_count = lax.axis_size("pair")
    virt_count = lax.axis_size("virt")
    ladder = ladder_block(amplitudes.astype(jnp.bfloat16), integrals, pair_count, virt_count)
    row_tiles = row_count // TR
    col_tiles = col_count // TC
    tile_total = row_tiles * col_tiles
    device_count = pair_count * virt_count
    per_peer = tile_total // device_count
    slots = partner_slot.reshape(tile_total)
    place = jnp.arange(tile_total, dtype=jnp.int32)
    earlier = (slots[None, :] == slots[:, None]) & (place[None, :] < place[:, None])
    inverse = slots * per_peer + jnp.sum(earlier.astype(jnp.int32), axis=1)
    hit = inverse[None, :] == place[:, None]
    ordering = jnp.sum(jnp.where(hit, place[None, :], 0), axis=1)
    weights = tile_mask.astype(jnp.float32)
    masked = ladder.reshape(row_tiles, TR, col_tiles, TC) * weights[:, None, :, None]
    tiles = masked.transpose(0, 2, 1, 3).reshape(tile_total, TR * TC)
    outgoing = jnp.take(tiles.astype(TILE_WIRE), ordering, axis=0)
    incoming = lax.all_to_all(
        outgoing.reshape(device_count, per_peer, TR * TC),
        ("pair", "virt"),
        split_axis=0,
        concat_axis=0,
        tiled=True,
    )
    partner = jnp.take(incoming.reshape(tile_total, TR * TC), inverse, axis=0)
    symmetric = (
        (tiles + partner.astype(jnp.float32))
        .reshape(row_tiles, col_tiles, TR, TC)
        .transpose(0, 2, 1, 3)
        .reshape(row_count, col_count)
    )
    denominator = occ_energy[:, None] + vir_energy[None, :]
    return amplitudes - symmetric / denominator


def solution(mesh):
    in_specs = (
        P("pair", "virt"),
        P("pair", "virt"),
        P("pair"),
        P("virt"),
        P("pair", "virt"),
        P("pair", "virt"),
    )
    out_specs = P("pair", "virt")
    return jax.shard_map(shards, mesh=mesh, in_specs=in_specs, out_specs=out_specs, check_vma=False)
```

```python
import functools
import jax
import jax.numpy as jnp
from jax import lax
from jax.experimental import pallas as pl
from jax.experimental.pallas import tpu as pltpu
from jax.sharding import PartitionSpec as P

TR = 8
TC = 128
CHUNK = 32
LAG_CORE = 1
LAG_DOT = 2
LAG_SUM = 4
WIRE = jnp.int16
TOP = 32767
BOUND = 6.0 * 0.046875
TILE_WIRE = jnp.float16
MESH = pl.DeviceIdType.MESH


def ladder_kernel(
    pairs, virts, chunks, rows, tile_n,
    amp_ref, int_ref, out_ref, chain_ref,
    weights, gathered, part_out, part_in, product,
    weight_sem, chain_send, chain_recv, plane_send, plane_recv,
    core_send, core_recv, part_send, part_recv,
):
    share = virts // pairs
    spots = pairs
    p = lax.axis_index("pair")
    v = lax.axis_index("virt")
    u = v // share
    c = v % share
    depth = amp_ref.shape[1]
    width = int_ref.shape[1]

    load = pltpu.make_async_copy(int_ref, weights, weight_sem)
    load.start()

    barrier = pltpu.get_barrier_semaphore()

    def greet(pp, vv):
        pl.semaphore_signal(barrier, inc=1, device_id=(pp, vv), device_id_type=MESH)

    for k in range(1, pairs):
        greet((p + k) % pairs, v)
    for k in range(1, share):
        greet(p, u * share + (c + k) % share)

    for k in range(1, spots):
        greet(p, (u + k) % spots * share + c)

    pl.semaphore_wait(barrier, pairs - 1 + share - 1 + spots - 1)

    def piece(r):
        return pl.ds(pl.multiple_of(r * rows, rows), rows)

    def chain_copy(src, w, r, up):
        return pltpu.make_async_remote_copy(
            src_ref=src,
            dst_ref=chain_ref.at[w, piece(r)],
            send_sem=chain_send.at[up, w, r],
            recv_sem=chain_recv.at[w, r],
            device_id=(p, v + share if up else v - share),
            device_id_type=MESH,
        )

    def plane_copy(src, w, r):
        return pltpu.make_async_remote_copy(
            src_ref=src,
            dst_ref=gathered.at[c, r, p],
            send_sem=plane_send.at[w, r],
            recv_sem=plane_recv.at[p, r],
            device_id=(w, v),
            device_id_type=MESH,
        )

    def keep_copy(src, r):
        return pltpu.make_async_copy(src, gathered.at[c, r, p], plane_recv.at[p, r])

    def pass_on(src, w, r):
        @pl.when(w != p)
        def _():
            plane_copy(src, w, r).start()

        @pl.when(w == p)
        def _():
            keep_copy(src, r).start()

    def core_copy(k, r):
        return pltpu.make_async_remote_copy(
            src_ref=gathered.at[c, r],
            dst_ref=gathered.at[c, r],
            send_sem=core_send.at[k, r],
            recv_sem=core_recv.at[k, r],
            device_id=(p, u * share + (c + k) % share),
            device_id_type=MESH,
        )

    def part_copy(q, r):
        return pltpu.make_async_remote_copy(
            src_ref=part_out.at[r, q],
            dst_ref=part_in.at[r, p],
            send_sem=part_send.at[q, r],
            recv_sem=part_recv.at[p, r],
            device_id=(q, v),
            device_id_type=MESH,
        )

    def spread(r):
        mine = amp_ref.at[piece(r)]

        @pl.when(u > 0)
        def _():
            chain_copy(mine, u, r, 0).start()

        @pl.when(u < spots - 1)
        def _():
            chain_copy(mine, u, r, 1).start()

        pass_on(mine, u, r)
        for d in range(1, spots):
            low = u - d
            high = u + d

            @pl.when(low >= 0)
            def _():
                chain_copy(mine, low, r, 1).wait_recv()
                block = chain_ref.at[low, piece(r)]

                @pl.when(u < spots - 1)
                def _():
                    chain_copy(block, low, r, 1).start()

                pass_on(block, low, r)

            @pl.when(high < spots)
            def _():
                chain_copy(mine, high, r, 0).wait_recv()
                block = chain_ref.at[high, piece(r)]

                @pl.when(u > 0)
                def _():
                    chain_copy(block, high, r, 0).start()

                pass_on(block, high, r)

    def swap(r):
        keep_copy(amp_ref.at[piece(r)], r).wait()
        for k in range(1, pairs):
            q = (p + k) % pairs
            pltpu.make_async_remote_copy(
                src_ref=amp_ref.at[piece(r)],
                dst_ref=gathered.at[c, r, q],
                send_sem=plane_send.at[q, r],
                recv_sem=plane_recv.at[q, r],
                device_id=(q, v),
                device_id_type=MESH,
            ).wait_recv()
        for k in range(1, share):
            core_copy(k, r).start()

    def multiply(r):
        for k in range(1, share):
            pltpu.make_async_remote_copy(
                src_ref=gathered.at[c, r],
                dst_ref=gathered.at[(c + share - k) % share, r],
                send_sem=core_send.at[k, r],
                recv_sem=core_recv.at[k, r],
                device_id=(p, u * share + (c + share - k) % share),
                device_id_type=MESH,
            ).wait_recv()

        @pl.when(r == 0)
        def _():
            load.wait()

        def columns(n, top):
            cut = pl.ds(pl.multiple_of(n * tile_n, tile_n), tile_n)
            total = jnp.zeros((pairs * rows, tile_n), jnp.float32)
            for s in range(share):
                total = total + jnp.dot(
                    gathered[s, r].reshape(pairs * rows, depth),
                    weights[s * depth : (s + 1) * depth, cut],
                    preferred_element_type=jnp.float32,
                )
            product[:, cut] = total
            for g in range(0, tile_n, TC):
                top = jnp.maximum(top, jnp.abs(total[:, g : g + TC]))
            return top

        top = lax.fori_loop(
            0, width // tile_n, columns, jnp.zeros((pairs * rows, TC), jnp.float32)
        )
        bound = share * depth * BOUND
        top = jnp.max(top, axis=1, keepdims=True)
        scale = jnp.clip(jnp.floor(top * (TOP / bound)) + 1.0, 1.0, float(TOP))
        inverse = (TOP * (TOP / bound)) / scale
        codes = jnp.broadcast_to(scale, (pairs * rows, TC)).astype(jnp.int32).astype(WIRE)
        for q in range(pairs):
            part_out[r, q, :, width:] = codes[q * rows : (q + 1) * rows]

        def encode(n, carry):
            cut = pl.ds(pl.multiple_of(n * tile_n, tile_n), tile_n)
            code = jnp.floor(product[:, cut] * inverse + 0.5)
            code = jnp.clip(code, -float(TOP), float(TOP)).astype(jnp.int32).astype(WIRE)
            for q in range(pairs):
                part_out[r, q, :, cut] = code[q * rows : (q + 1) * rows]
            return carry

        lax.fori_loop(0, width // tile_n, encode, 0)
        out_ref[piece(r), :] = product[pl.ds(pl.multiple_of(p * rows, rows), rows), :]
        for k in range(1, pairs):
            part_copy((p + k) % pairs, r).start()

    def collect(r):
        for k in range(1, pairs):
            q = (p + k) % pairs
            pltpu.make_async_remote_copy(
                src_ref=part_out.at[r, q],
                dst_ref=part_in.at[r, q],
                send_sem=part_send.at[q, r],
                recv_sem=part_recv.at[q, r],
                device_id=(q, v),
                device_id_type=MESH,
            ).wait_recv()
        unit = share * depth * BOUND / TOP / TOP
        total = out_ref[piece(r), :]
        for k in range(1, pairs):
            q = (p + k) % pairs
            scale = part_in[r, q, :, width:].astype(jnp.int32).astype(jnp.float32)[:, :1]
            code = part_in[r, q, :, :width].astype(jnp.int32).astype(jnp.float32)
            total = total + code * (scale * unit)
        out_ref[piece(r), :] = total

    def step(s, carry):
        @pl.when(s < chunks)
        def _():
            spread(s)

        @pl.when((s >= LAG_CORE) & (s < chunks + LAG_CORE))
        def _():
            swap(s - LAG_CORE)

        @pl.when((s >= LAG_DOT) & (s < chunks + LAG_DOT))
        def _():
            multiply(s - LAG_DOT)

        @pl.when(s >= LAG_SUM)
        def _():
            collect(s - LAG_SUM)

        return carry

    lax.fori_loop(0, chunks + LAG_SUM, step, 0)

    def drain(r, carry):
        mine = amp_ref.at[piece(r)]
        for w in range(spots):
            @pl.when((u > 0) & (w >= u))
            def _():
                chain_copy(mine, w, r, 0).wait_send()

            @pl.when((u < spots - 1) & (w <= u))
            def _():
                chain_copy(mine, w, r, 1).wait_send()

            @pl.when(w != p)
            def _():
                plane_copy(mine, w, r).wait_send()
                part_copy(w, r).wait_send()
        for k in range(1, share):
            core_copy(k, r).wait_send()
        return carry

    lax.fori_loop(0, chunks, drain, 0)


def ladder_block(amp_half, integrals, pairs, virts):
    row_count, depth = amp_half.shape
    width = integrals.shape[1]
    rows = min(CHUNK, row_count)
    chunks = row_count // rows
    share = virts // pairs
    tile_n = min(256, width)
    dma = pltpu.SemaphoreType.DMA
    ladder, _ = pl.pallas_call(
        functools.partial(ladder_kernel, pairs, virts, chunks, rows, tile_n),
        out_shape=(
            jax.ShapeDtypeStruct((row_count, width), jnp.float32),
            jax.ShapeDtypeStruct((pairs, row_count, depth), jnp.bfloat16),
        ),
        in_specs=[pl.BlockSpec(memory_space=pl.ANY)] * 2,
        out_specs=(
            pl.BlockSpec(memory_space=pltpu.VMEM),
            pl.BlockSpec(memory_space=pl.ANY),
        ),
        scratch_shapes=[
            pltpu.VMEM(integrals.shape, jnp.bfloat16),
            pltpu.VMEM((share, chunks, pairs, rows, depth), jnp.bfloat16),
            pltpu.VMEM((chunks, pairs, rows, width + TC), WIRE),
            pltpu.VMEM((chunks, pairs, rows, width + TC), WIRE),
            pltpu.VMEM((pairs * rows, width), jnp.float32),
            dma(()),
            dma((2, pairs, chunks)),
            dma((pairs, chunks)),
            dma((pairs, chunks)),
            dma((pairs, chunks)),
            dma((share, chunks)),
            dma((share, chunks)),
            dma((pairs, chunks)),
            dma((pairs, chunks)),
        ],
        compiler_params=pltpu.CompilerParams(
            collective_id=0, has_side_effects=True, vmem_limit_bytes=60 * 2**20
        ),
        cost_estimate=pl.CostEstimate(
            flops=2 * pairs * row_count * share * depth * width,
            bytes_accessed=2 * integrals.size + 8 * amp_half.size,
            transcendentals=0,
        ),
    )(amp_half, integrals)
    return ladder


def shards(amplitudes, integrals, occ_energy, vir_energy, tile_mask, partner_slot):
    row_count, col_count = amplitudes.shape
    pair_count = lax.axis_size("pair")
    virt_count = lax.axis_size("virt")
    ladder = ladder_block(amplitudes.astype(jnp.bfloat16), integrals, pair_count, virt_count)
    row_tiles = row_count // TR
    col_tiles = col_count // TC
    tile_total = row_tiles * col_tiles
    device_count = pair_count * virt_count
    per_peer = tile_total // device_count
    slots = partner_slot.reshape(tile_total)
    place = jnp.arange(tile_total, dtype=jnp.int32)
    earlier = (slots[None, :] == slots[:, None]) & (place[None, :] < place[:, None])
    inverse = slots * per_peer + jnp.sum(earlier.astype(jnp.int32), axis=1)
    hit = inverse[None, :] == place[:, None]
    ordering = jnp.sum(jnp.where(hit, place[None, :], 0), axis=1)
    weights = tile_mask.astype(jnp.float32)
    masked = ladder.reshape(row_tiles, TR, col_tiles, TC) * weights[:, None, :, None]
    tiles = masked.transpose(0, 2, 1, 3).reshape(tile_total, TR * TC)
    outgoing = jnp.take(tiles.astype(TILE_WIRE), ordering, axis=0)
    incoming = lax.all_to_all(
        outgoing.reshape(device_count, per_peer, TR * TC),
        ("pair", "virt"),
        split_axis=0,
        concat_axis=0,
        tiled=True,
    )
    partner = jnp.take(incoming.reshape(tile_total, TR * TC), inverse, axis=0)
    symmetric = (
        (tiles + partner.astype(jnp.float32))
        .reshape(row_tiles, col_tiles, TR, TC)
        .transpose(0, 2, 1, 3)
        .reshape(row_count, col_count)
    )
    denominator = occ_energy[:, None] + vir_energy[None, :]
    return amplitudes - symmetric / denominator


def solution(mesh):
    in_specs = (
        P("pair", "virt"),
        P("pair", "virt"),
        P("pair"),
        P("virt"),
        P("pair", "virt"),
        P("pair", "virt"),
    )
    out_specs = P("pair", "virt")
    return jax.shard_map(shards, mesh=mesh, in_specs=in_specs, out_specs=out_specs, check_vma=False)
```

```python
import functools
import jax
import jax.numpy as jnp
from jax import lax
from jax.experimental import pallas as pl
from jax.experimental.pallas import tpu as pltpu
from jax.sharding import PartitionSpec as P

TR = 8
TC = 128
CHUNK = 128
LAG_CORE = 1
LAG_DOT = 2
LAG_SUM = 3
WIRE = jnp.int16
TOP = 32767
BOUND = 6.0 * 0.046875
TILE_WIRE = jnp.float16
MESH = pl.DeviceIdType.MESH


def ladder_kernel(
    pairs, virts, chunks, rows, tile_n,
    amp_ref, int_ref, out_ref, chain_ref,
    weights, gathered, part_out, part_in, product,
    weight_sem, chain_send, chain_recv, plane_send, plane_recv,
    core_send, core_recv, part_send, part_recv,
):
    share = virts // pairs
    spots = pairs
    p = lax.axis_index("pair")
    v = lax.axis_index("virt")
    u = v // share
    c = v % share
    depth = amp_ref.shape[1]
    width = int_ref.shape[1]

    load = pltpu.make_async_copy(int_ref, weights, weight_sem)
    load.start()

    barrier = pltpu.get_barrier_semaphore()

    def greet(pp, vv):
        pl.semaphore_signal(barrier, inc=1, device_id=(pp, vv), device_id_type=MESH)

    for k in range(1, pairs):
        greet((p + k) % pairs, v)
    for k in range(1, share):
        greet(p, u * share + (c + k) % share)

    for k in range(1, spots):
        greet(p, (u + k) % spots * share + c)

    pl.semaphore_wait(barrier, pairs - 1 + share - 1 + spots - 1)

    def piece(r):
        return pl.ds(pl.multiple_of(r * rows, rows), rows)

    def chain_copy(src, w, r, up):
        return pltpu.make_async_remote_copy(
            src_ref=src,
            dst_ref=chain_ref.at[w, piece(r)],
            send_sem=chain_send.at[up, w, r],
            recv_sem=chain_recv.at[w, r],
            device_id=(p, v + share if up else v - share),
            device_id_type=MESH,
        )

    def plane_copy(src, w, r):
        return pltpu.make_async_remote_copy(
            src_ref=src,
            dst_ref=gathered.at[c, r, p],
            send_sem=plane_send.at[w, r],
            recv_sem=plane_recv.at[p, r],
            device_id=(w, v),
            device_id_type=MESH,
        )

    def keep_copy(src, r):
        return pltpu.make_async_copy(src, gathered.at[c, r, p], plane_recv.at[p, r])

    def pass_on(src, w, r):
        @pl.when(w != p)
        def _():
            plane_copy(src, w, r).start()

        @pl.when(w == p)
        def _():
            keep_copy(src, r).start()

    def core_copy(k, r):
        return pltpu.make_async_remote_copy(
            src_ref=gathered.at[c, r],
            dst_ref=gathered.at[c, r],
            send_sem=core_send.at[k, r],
            recv_sem=core_recv.at[k, r],
            device_id=(p, u * share + (c + k) % share),
            device_id_type=MESH,
        )

    def part_copy(q, r):
        return pltpu.make_async_remote_copy(
            src_ref=part_out.at[r, q],
            dst_ref=part_in.at[r, p],
            send_sem=part_send.at[q, r],
            recv_sem=part_recv.at[p, r],
            device_id=(q, v),
            device_id_type=MESH,
        )

    def spread(r):
        mine = amp_ref.at[piece(r)]

        @pl.when(u > 0)
        def _():
            chain_copy(mine, u, r, 0).start()

        @pl.when(u < spots - 1)
        def _():
            chain_copy(mine, u, r, 1).start()

        pass_on(mine, u, r)
        for d in range(1, spots):
            low = u - d
            high = u + d

            @pl.when(low >= 0)
            def _():
                chain_copy(mine, low, r, 1).wait_recv()
                block = chain_ref.at[low, piece(r)]

                @pl.when(u < spots - 1)
                def _():
                    chain_copy(block, low, r, 1).start()

                pass_on(block, low, r)

            @pl.when(high < spots)
            def _():
                chain_copy(mine, high, r, 0).wait_recv()
                block = chain_ref.at[high, piece(r)]

                @pl.when(u > 0)
                def _():
                    chain_copy(block, high, r, 0).start()

                pass_on(block, high, r)

    def swap(r):
        keep_copy(amp_ref.at[piece(r)], r).wait()
        for k in range(1, pairs):
            q = (p + k) % pairs
            pltpu.make_async_remote_copy(
                src_ref=amp_ref.at[piece(r)],
                dst_ref=gathered.at[c, r, q],
                send_sem=plane_send.at[q, r],
                recv_sem=plane_recv.at[q, r],
                device_id=(q, v),
                device_id_type=MESH,
            ).wait_recv()
        for k in range(1, share):
            core_copy(k, r).start()

    def multiply(r):
        for k in range(1, share):
            pltpu.make_async_remote_copy(
                src_ref=gathered.at[c, r],
                dst_ref=gathered.at[(c + share - k) % share, r],
                send_sem=core_send.at[k, r],
                recv_sem=core_recv.at[k, r],
                device_id=(p, u * share + (c + share - k) % share),
                device_id_type=MESH,
            ).wait_recv()

        @pl.when(r == 0)
        def _():
            load.wait()

        def columns(n, top):
            cut = pl.ds(pl.multiple_of(n * tile_n, tile_n), tile_n)
            total = jnp.zeros((pairs * rows, tile_n), jnp.float32)
            for s in range(share):
                total = total + jnp.dot(
                    gathered[s, r].reshape(pairs * rows, depth),
                    weights[s * depth : (s + 1) * depth, cut],
                    preferred_element_type=jnp.float32,
                )
            product[:, cut] = total
            for g in range(0, tile_n, TC):
                top = jnp.maximum(top, jnp.abs(total[:, g : g + TC]))
            return top

        top = lax.fori_loop(
            0, width // tile_n, columns, jnp.zeros((pairs * rows, TC), jnp.float32)
        )
        bound = share * depth * BOUND
        top = jnp.max(top, axis=1, keepdims=True)
        scale = jnp.clip(jnp.floor(top * (TOP / bound)) + 1.0, 1.0, float(TOP))
        inverse = (TOP * (TOP / bound)) / scale
        codes = jnp.broadcast_to(scale, (pairs * rows, TC)).astype(jnp.int32).astype(WIRE)
        for q in range(pairs):
            part_out[r, q, :, width:] = codes[q * rows : (q + 1) * rows]

        def encode(n, carry):
            cut = pl.ds(pl.multiple_of(n * tile_n, tile_n), tile_n)
            code = jnp.floor(product[:, cut] * inverse + 0.5)
            code = jnp.clip(code, -float(TOP), float(TOP)).astype(jnp.int32).astype(WIRE)
            for q in range(pairs):
                part_out[r, q, :, cut] = code[q * rows : (q + 1) * rows]
            return carry

        lax.fori_loop(0, width // tile_n, encode, 0)
        out_ref[piece(r), :] = product[pl.ds(pl.multiple_of(p * rows, rows), rows), :]
        for k in range(1, pairs):
            part_copy((p + k) % pairs, r).start()

    def collect(r):
        for k in range(1, pairs):
            q = (p + k) % pairs
            pltpu.make_async_remote_copy(
                src_ref=part_out.at[r, q],
                dst_ref=part_in.at[r, q],
                send_sem=part_send.at[q, r],
                recv_sem=part_recv.at[q, r],
                device_id=(q, v),
                device_id_type=MESH,
            ).wait_recv()
        unit = share * depth * BOUND / TOP / TOP
        total = out_ref[piece(r), :]
        for k in range(1, pairs):
            q = (p + k) % pairs
            scale = part_in[r, q, :, width:].astype(jnp.int32).astype(jnp.float32)[:, :1]
            code = part_in[r, q, :, :width].astype(jnp.int32).astype(jnp.float32)
            total = total + code * (scale * unit)
        out_ref[piece(r), :] = total

    def step(s, carry):
        @pl.when(s < chunks)
        def _():
            spread(s)

        @pl.when((s >= LAG_CORE) & (s < chunks + LAG_CORE))
        def _():
            swap(s - LAG_CORE)

        @pl.when((s >= LAG_DOT) & (s < chunks + LAG_DOT))
        def _():
            multiply(s - LAG_DOT)

        @pl.when(s >= LAG_SUM)
        def _():
            collect(s - LAG_SUM)

        return carry

    lax.fori_loop(0, chunks + LAG_SUM, step, 0)

    def drain(r, carry):
        mine = amp_ref.at[piece(r)]
        for w in range(spots):
            @pl.when((u > 0) & (w >= u))
            def _():
                chain_copy(mine, w, r, 0).wait_send()

            @pl.when((u < spots - 1) & (w <= u))
            def _():
                chain_copy(mine, w, r, 1).wait_send()

            @pl.when(w != p)
            def _():
                plane_copy(mine, w, r).wait_send()
                part_copy(w, r).wait_send()
        for k in range(1, share):
            core_copy(k, r).wait_send()
        return carry

    lax.fori_loop(0, chunks, drain, 0)


def ladder_block(amp_half, integrals, pairs, virts):
    row_count, depth = amp_half.shape
    width = integrals.shape[1]
    rows = min(CHUNK, row_count)
    chunks = row_count // rows
    share = virts // pairs
    tile_n = min(256, width)
    dma = pltpu.SemaphoreType.DMA
    ladder, _ = pl.pallas_call(
        functools.partial(ladder_kernel, pairs, virts, chunks, rows, tile_n),
        out_shape=(
            jax.ShapeDtypeStruct((row_count, width), jnp.float32),
            jax.ShapeDtypeStruct((pairs, row_count, depth), jnp.bfloat16),
        ),
        in_specs=[pl.BlockSpec(memory_space=pl.ANY)] * 2,
        out_specs=(
            pl.BlockSpec(memory_space=pltpu.VMEM),
            pl.BlockSpec(memory_space=pl.ANY),
        ),
        scratch_shapes=[
            pltpu.VMEM(integrals.shape, jnp.bfloat16),
            pltpu.VMEM((share, chunks, pairs, rows, depth), jnp.bfloat16),
            pltpu.VMEM((chunks, pairs, rows, width + TC), WIRE),
            pltpu.VMEM((chunks, pairs, rows, width + TC), WIRE),
            pltpu.VMEM((pairs * rows, width), jnp.float32),
            dma(()),
            dma((2, pairs, chunks)),
            dma((pairs, chunks)),
            dma((pairs, chunks)),
            dma((pairs, chunks)),
            dma((share, chunks)),
            dma((share, chunks)),
            dma((pairs, chunks)),
            dma((pairs, chunks)),
        ],
        compiler_params=pltpu.CompilerParams(
            collective_id=0, has_side_effects=True, vmem_limit_bytes=60 * 2**20
        ),
        cost_estimate=pl.CostEstimate(
            flops=2 * pairs * row_count * share * depth * width,
            bytes_accessed=2 * integrals.size + 8 * amp_half.size,
            transcendentals=0,
        ),
    )(amp_half, integrals)
    return ladder


def shards(amplitudes, integrals, occ_energy, vir_energy, tile_mask, partner_slot):
    row_count, col_count = amplitudes.shape
    pair_count = lax.axis_size("pair")
    virt_count = lax.axis_size("virt")
    ladder = ladder_block(amplitudes.astype(jnp.bfloat16), integrals, pair_count, virt_count)
    row_tiles = row_count // TR
    col_tiles = col_count // TC
    tile_total = row_tiles * col_tiles
    device_count = pair_count * virt_count
    per_peer = tile_total // device_count
    slots = partner_slot.reshape(tile_total)
    place = jnp.arange(tile_total, dtype=jnp.int32)
    earlier = (slots[None, :] == slots[:, None]) & (place[None, :] < place[:, None])
    inverse = slots * per_peer + jnp.sum(earlier.astype(jnp.int32), axis=1)
    hit = inverse[None, :] == place[:, None]
    ordering = jnp.sum(jnp.where(hit, place[None, :], 0), axis=1)
    weights = tile_mask.astype(jnp.float32)
    masked = ladder.reshape(row_tiles, TR, col_tiles, TC) * weights[:, None, :, None]
    tiles = masked.transpose(0, 2, 1, 3).reshape(tile_total, TR * TC)
    outgoing = jnp.take(tiles.astype(TILE_WIRE), ordering, axis=0)
    incoming = lax.all_to_all(
        outgoing.reshape(device_count, per_peer, TR * TC),
        ("pair", "virt"),
        split_axis=0,
        concat_axis=0,
        tiled=True,
    )
    partner = jnp.take(incoming.reshape(tile_total, TR * TC), inverse, axis=0)
    symmetric = (
        (tiles + partner.astype(jnp.float32))
        .reshape(row_tiles, col_tiles, TR, TC)
        .transpose(0, 2, 1, 3)
        .reshape(row_count, col_count)
    )
    denominator = occ_energy[:, None] + vir_energy[None, :]
    return amplitudes - symmetric / denominator


def solution(mesh):
    in_specs = (
        P("pair", "virt"),
        P("pair", "virt"),
        P("pair"),
        P("virt"),
        P("pair", "virt"),
        P("pair", "virt"),
    )
    out_specs = P("pair", "virt")
    return jax.shard_map(shards, mesh=mesh, in_specs=in_specs, out_specs=out_specs, check_vma=False)
```
